32 devices in a mesh: groups: 2 (over x), pool: 16 (over z, y, core).
Axes of the slice: x: 2, y: 2, z: 4, core: 2. Of those that a mesh axis runs over, the one named last changes fastest.
Arguments:
- hidden: bfloat16 [512, 8192], P(('groups', 'pool')), parts along dimension 0, may hold values from -450 to 450
- attention_norm_scale: bfloat16 [8192], replicated, may hold values from 0.25 to 1.75
- query_weight_matrix: bfloat16 [8192, 8192], P(None, 'pool'), may hold values from -0.0625 to 0.0625
- adapter_down_weight: bfloat16 [8192, 4096], P(None, ('groups', 'pool')), parts along dimension 1, may hold values from -0.0625 to 0.0625
- adapter_up_weight: bfloat16 [4096, 8192], P('groups', 'pool'), parts along dimension 0, may hold values from -0.75 to 0.75
- row_adapter_index: int32 [512], P(('groups', 'pool')), parts along dimension 0, may hold values from 0 to 31, as said below
- request_pool_index: int32 [1536], P(('groups', 'pool')), parts along dimension 0, may hold values from 0 to 256, as said below
Outputs:
- query: bfloat16 [512, 8192], P('groups', 'pool'), parts along dimension 0
The draws below stay inside these ranges and needn't reach their ends.
There are 2 independent parts, one for each index of `groups`. The reference program is written for one: setup_inputs(seed, part) draws one part's arguments, and reference() takes and returns one part's arrays. A program takes and returns all parts, laid end to end along the dimension named above; an argument that names none is the same for every part. Nothing has to cross between parts.
Inputs may be any that keep to these rules, and one draw needn't show every extreme that they name: `row_adapter_index`: the adapters p * 2 to (p + 1) * 2 - 1 of one pool index p are named by at most 48 rows in all, and by exactly 48 rows for one p. `request_pool_index`: list p (entries p * 48 to (p + 1) * 48 - 1) holds in increasing order every row whose row_adapter_index lies in p * 2 to (p + 1) * 2 - 1, then 256 in the slots left; one list has no such slot.
All inputs are finite; a program needn't handle non-finite values.
Results may differ from the reference program's by a relative error of at most 0.0054.
Values may be sent and summed in bfloat16 or wider, within the bound.
A program may use at most 64 MiB of HBM per device.

```python
import math
import jax
import jax.numpy as jnp
from jax import lax

MODEL_WIDTH = 8192
ADAPTER_RANK = 64
ADP_DEV = 2
ADAPTER_TOTAL = 32
ROWS = 256
MAXREQ = 48
N_POOL = 16


def owner_plan(key):
    key_hot, key_tickets, key_shuffle = jax.random.split(key, 3)
    hot_owner = jax.random.randint(key_hot, (), 0, N_POOL)
    tickets = jax.random.permutation(key_tickets, (N_POOL - 1) * MAXREQ)[:ROWS - MAXREQ]
    others = (hot_owner + 1 + tickets // MAXREQ) % N_POOL
    assigned = jnp.concatenate([jnp.full((MAXREQ,), hot_owner, jnp.int32), others.astype(jnp.int32)])
    shuffle = jax.random.permutation(key_shuffle, ROWS)
    return assigned[shuffle].astype(jnp.int32)


def draw_row_adapter_index(key, part):
    row_owner = owner_plan(key)
    key = jax.random.fold_in(key, 5)
    local_slot = jax.random.randint(key, (ROWS,), 0, ADP_DEV)
    return (row_owner * ADP_DEV + local_slot).astype(jnp.int32)


def draw_request_pool_index(key, part):
    row_owner = owner_plan(key)
    row_iota = jnp.arange(ROWS, dtype=jnp.int32)
    matches = row_owner[None, :] == jnp.arange(N_POOL, dtype=jnp.int32)[:, None]
    position = jnp.cumsum(matches.astype(jnp.int32), axis=1) - 1
    slot_iota = jnp.arange(MAXREQ, dtype=jnp.int32)[None, None, :]
    hits = matches[:, :, None] & (position[:, :, None] == slot_iota)
    present = jnp.any(hits, axis=1)
    selected_factors = jnp.sum(jnp.where(hits, row_iota[None, :, None], 0), axis=1)
    compact = jnp.where(present, selected_factors, ROWS)
    return compact.reshape(-1).astype(jnp.int32)


def draw_hidden(key, part):
    key = jax.random.fold_in(key, 11)
    key_noise, key_rows, key_cols = jax.random.split(key, 3)
    row_scale = jnp.exp(jax.random.uniform(key_rows, (ROWS, 1), jnp.float32) * math.log(10.0))
    col_scale = jnp.exp(jax.random.uniform(key_cols, (1, MODEL_WIDTH), jnp.float32) * math.log(10.0))
    noise = jnp.clip(jax.random.normal(key_noise, (ROWS, MODEL_WIDTH), jnp.float32), -5.0, 5.0)
    return (noise * row_scale * col_scale * 0.3).astype(jnp.bfloat16)


def shard_levels(stream_key, shape, cuts, least, high):
    loudness, own = 1.0, jax.random.fold_in(stream_key, 6)
    for dim, shards_of in cuts:
        draws = jnp.exp(jax.random.uniform(jax.random.fold_in(own, dim), (shards_of,), jnp.float32, least / len(cuts), high / len(cuts)))
        loudness = loudness * jnp.repeat(draws, shape[dim] // shards_of).reshape([-1 if axis == dim else 1 for axis in range(len(shape))])
    return loudness


def centred(stream_key, shape, deviation, bound, shards=(), kind=jnp.bfloat16):
    level = shard_levels(stream_key, shape, shards, -0.22, 0.18) if shards else 1.0
    result = jax.random.normal(stream_key, shape, jnp.float32) * deviation * level
    return jnp.minimum(jnp.maximum(result, -bound), bound).astype(kind)


def setup_inputs(seed: int = 0, part: int = 0) -> dict:
    streams_of = jax.random.split(jax.random.key(seed), 8)
    own_keys = jax.random.split(jax.random.fold_in(streams_of[7], part), 8)
    hidden = draw_hidden(jax.random.fold_in(jax.random.fold_in(streams_of[7], part), 71), part)
    attention_norm_scale = jnp.clip(1.0 + 0.15 * jax.random.normal(streams_of[1], (MODEL_WIDTH,), jnp.float32), 0.25, 1.75).astype(jnp.bfloat16)
    query_weight_matrix = centred(streams_of[2], (MODEL_WIDTH, MODEL_WIDTH), MODEL_WIDTH ** -0.5, 0.0625, ((1, 16),))
    adapter_down_weight = centred(own_keys[3], (MODEL_WIDTH, ADAPTER_TOTAL * ADAPTER_RANK), MODEL_WIDTH ** -0.5, 0.0625, ((1, 16),))
    adapter_up_weight = centred(own_keys[4], (ADAPTER_TOTAL * ADAPTER_RANK, MODEL_WIDTH), ADAPTER_RANK ** -0.5, 0.75, ((1, 16),))
    row_adapter_index = draw_row_adapter_index(jax.random.fold_in(jax.random.fold_in(streams_of[7], part), 71), part)
    request_pool_index = draw_request_pool_index(jax.random.fold_in(jax.random.fold_in(streams_of[7], part), 71), part)
    return {"hidden": hidden, "attention_norm_scale": attention_norm_scale, "query_weight_matrix": query_weight_matrix, "adapter_down_weight": adapter_down_weight, "adapter_up_weight": adapter_up_weight, "row_adapter_index": row_adapter_index, "request_pool_index": request_pool_index}


def rms_scaled(row_values, gain_vec):
    values = row_values.astype(jnp.float32)
    mean_square = lax.optimization_barrier(jnp.mean(values * values, axis=-1, keepdims=True))
    return (values * lax.rsqrt(mean_square + 1e-05) * gain_vec.astype(jnp.float32)).astype(jnp.bfloat16)

def reference(hidden, attention_norm_scale, query_weight_matrix, adapter_down_weight, adapter_up_weight, row_adapter_index, request_pool_index):
    normed = rms_scaled(hidden, attention_norm_scale)
    query_output = jnp.dot(normed, query_weight_matrix, preferred_element_type=jnp.float32)
    total_row_number = normed.shape[0]
    entries = request_pool_index.shape[0]
    row_tile_count = 32
    owner_of = (jnp.arange(entries, dtype=jnp.int32) // MAXREQ).astype(jnp.int32)
    usable = request_pool_index < total_row_number
    safe_rows = jnp.where(usable, request_pool_index, 0).astype(jnp.int32)
    chosen = jnp.take(row_adapter_index, safe_rows, axis=0).astype(jnp.int32)
    is_owned = usable & (chosen // ADP_DEV == owner_of)
    down_lookup_table = adapter_down_weight.reshape(MODEL_WIDTH, ADAPTER_TOTAL, ADAPTER_RANK)

    def shrink(inputs):
        row_block, id_block = inputs
        a_pick = jnp.take(down_lookup_table, id_block, axis=1).astype(jnp.float32)
        return jnp.einsum('rd,drk->rk', row_block.astype(jnp.float32), a_pick)
    selected_factors = jnp.take(normed, safe_rows, axis=0).reshape(-1, row_tile_count, MODEL_WIDTH)
    low_rank = lax.map(shrink, (selected_factors, chosen.reshape(-1, row_tile_count))).reshape(entries, ADAPTER_RANK)
    low_rank = jnp.where(is_owned[:, None], low_rank, 0.0).astype(jnp.bfloat16)
    target = jnp.where(is_owned, safe_rows, total_row_number).astype(jnp.int32)
    factor_pair = jnp.zeros((total_row_number, ADAPTER_RANK), jnp.float32).at[target].add(low_rank.astype(jnp.float32), mode='drop')
    factor_pair = lax.optimization_barrier(factor_pair.astype(jnp.bfloat16)).astype(jnp.float32)
    up_lookup_table = adapter_up_weight.reshape(ADAPTER_TOTAL, ADAPTER_RANK, MODEL_WIDTH)

    def widen_rows(inputs):
        factor_block, id_block = inputs
        b_pick = jnp.take(up_lookup_table, id_block, axis=0).astype(jnp.float32)
        return jnp.einsum('rk,rkd->rd', factor_block, b_pick)
    adapter_update = lax.map(widen_rows, (factor_pair.reshape(-1, row_tile_count, ADAPTER_RANK), row_adapter_index.reshape(-1, row_tile_count))).reshape(total_row_number, MODEL_WIDTH)
    return (query_output + adapter_update).astype(jnp.bfloat16)
```

```python
import functools

import jax
import jax.numpy as jnp
from jax import lax
from jax.experimental import pallas as pl
from jax.experimental.pallas import tpu as pltpu
from jax.sharding import PartitionSpec as P

ADAPTER_RANK = 64
ADP_DEV = 2
SLOTS = 64
HALF = SLOTS // 2
CHUNKS = 8
AHEAD = 2
MESH = pl.DeviceIdType.MESH
F32, BF16 = jnp.float32, jnp.bfloat16


def each(n, body):
    if n <= 8:
        for i in range(n):
            body(i)
    else:

        def step(i, carry):
            body(i)
            return carry

        lax.fori_loop(0, n, step, 0)


def kernel(
    nz, ny, h_hbm, g_ref, w_hbm, d_hbm, u_hbm, ids_ref, list_ref, out_ref,
    x, w, d, u, h, acc, accd, meta, comp, expand, idcol, wide,
    h_sem, w_sem, d_sem, u_sem, z_send, y_send, s_send, recv, m_send, m_recv, c_send, c_recv,
):
    pool = nz * ny * 2
    block, width = h_hbm.shape
    rows = block * pool
    kc = width // CHUNKS
    tile = min(rows, 256)
    me = lax.axis_index("pool")
    c = lax.rem(me, 2)
    y = lax.rem(me // 2, ny)
    z = me // (2 * ny)

    def pid(zz, yy, cc):
        return (zz * ny + yy) * 2 + cc

    load_h = pltpu.make_async_copy(h_hbm, h, h_sem)
    load_h.start()

    barrier = pltpu.get_barrier_semaphore()

    def greet(i):
        pl.semaphore_signal(
            barrier, inc=1, device_id={"pool": lax.rem(me + 1 + i, pool)}, device_id_type=MESH
        )

    each(pool - 1, greet)

    mine8 = pl.ds(pl.multiple_of(me * 8, 8), 8)
    meta[mine8, :] = jnp.full((8, 128), -1, jnp.int32)
    meta[pl.ds(me * 8, 1), pl.ds(0, block)] = ids_ref[...].reshape(1, block)
    entries = list_ref.shape[0]
    meta[pl.ds(me * 8 + 1, 1), pl.ds(0, entries)] = list_ref[...].reshape(1, entries)

    def cols(k):
        return pl.ds(pl.multiple_of(k * kc, kc), kc)

    def load_w(k):
        return pltpu.make_async_copy(w_hbm.at[cols(k), :], w.at[cols(k), :], w_sem.at[k])

    def load_d(k):
        return pltpu.make_async_copy(d_hbm.at[cols(k), :], d.at[cols(k), :], d_sem.at[k])

    load_u = pltpu.make_async_copy(u_hbm, u, u_sem)

    load_h.wait()
    for k in range(CHUNKS):
        load_d(k).start()
        load_w(k).start()
    load_u.start()

    total = jnp.zeros((block, 128), F32)
    for k in range(CHUNKS):
        v = h[:, k * kc : (k + 1) * kc].astype(F32)
        v = v * v
        for j in range(kc // 128):
            total = total + v[:, j * 128 : (j + 1) * 128]
    mean = jnp.sum(total, axis=1, keepdims=True) / width
    scale = lax.rsqrt(mean + 1e-05)
    mine = pl.ds(pl.multiple_of(me * block, block), block)
    for k in range(CHUNKS):
        v = h[:, k * kc : (k + 1) * kc].astype(F32)
        g = g_ref[:, k * kc : (k + 1) * kc].astype(F32)
        x[mine, k * kc : (k + 1) * kc] = (v * scale * g).astype(BF16)

    pl.semaphore_wait(barrier, pool - 1)

    def piece(src, k):
        return x.at[pl.ds(pl.multiple_of(src * block, block), block), cols(k)]

    def push(src, k, sem, target):
        return pltpu.make_async_remote_copy(
            src_ref=piece(src, k),
            dst_ref=piece(src, k),
            send_sem=sem,
            recv_sem=recv.at[k, src],
            device_id={"pool": target},
            device_id_type=MESH,
        )

    def to_z(k, i):
        zz = lax.rem(z + 1 + i, nz)
        return push(me, k, z_send.at[k, i], pid(zz, y, c))

    def to_y(k, zz, i):
        yy = lax.rem(y + 1 + i, ny)
        return push(pid(zz, y, c), k, y_send.at[k, zz * max(ny - 1, 1) + i], pid(z, yy, c))

    def to_s(k, zz, yy):
        return push(pid(zz, yy, c), k, s_send.at[k, zz * ny + yy], pid(z, y, 1 - c))

    def arrived(k, src):
        push(src, k, z_send.at[0, 0], pid(z, y, 1 - c)).wait_recv()

    def own(k):
        each(ny - 1, lambda i: to_y(k, z, i).start())
        each(nz - 1, lambda i: to_z(k, i).start())
        to_s(k, z, y).start()

    for k in range(AHEAD):
        own(k)

    def tell(i):
        q = lax.rem(me + 1 + i, pool)
        return pltpu.make_async_remote_copy(
            src_ref=meta.at[mine8, :],
            dst_ref=meta.at[mine8, :],
            send_sem=m_send.at[i],
            recv_sem=m_recv.at[me],
            device_id={"pool": q},
            device_id_type=MESH,
        )

    each(pool - 1, lambda i: tell(i).start())

    acc[...] = jnp.zeros_like(acc)
    accd[...] = jnp.zeros_like(accd)

    def down(k):
        load_d(k).wait()

        def part(t):
            at = pl.ds(pl.multiple_of(t * tile, tile), tile)
            accd[at, :] += jnp.dot(x[at, cols(k)], d[cols(k), :], preferred_element_type=F32)

        each(rows // tile, part)

    def base(k):
        load_w(k).wait()

        def part(t):
            at = pl.ds(pl.multiple_of(t * tile, tile), tile)
            acc[at, :] += jnp.dot(x[at, cols(k)], w[cols(k), :], preferred_element_type=F32)

        each(rows // tile, part)

    def step(i, carry):
        @pl.when(i + AHEAD < CHUNKS)
        def _():
            own(i + AHEAD)

        @pl.when(i < CHUNKS)
        def _():
            def from_z(j):
                zz = lax.rem(z + 1 + j, nz)
                arrived(i, pid(zz, y, c))
                each(ny - 1, lambda t: to_y(i, zz, t).start())
                to_s(i, zz, y).start()

            each(nz - 1, from_z)

        @pl.when((i >= 1) & (i <= CHUNKS))
        def _():
            def from_y(t):
                yy = lax.rem(y + 1 + t, ny)

                def at_z(j):
                    zz = lax.rem(z + j, nz)
                    arrived(i - 1, pid(zz, yy, c))
                    to_s(i - 1, zz, yy).start()

                each(nz, at_z)

            each(ny - 1, from_y)

        @pl.when(i >= 2)
        def _():
            each(nz * ny, lambda q: arrived(i - 2, q * 2 + 1 - c))
            down(i - 2)

            @pl.when(i - 2 < CHUNKS - 1)
            def _():
                base(i - 2)

        @pl.when(i == 1)
        def _():
            tables()

        return carry

    def tables():
        def got(i):
            q = lax.rem(me + 1 + i, pool)
            at = pl.ds(pl.multiple_of(q * 8, 8), 8)
            pltpu.make_async_remote_copy(
                src_ref=meta.at[at, :], dst_ref=meta.at[at, :], send_sem=m_send.at[0],
                recv_sem=m_recv.at[q], device_id={"pool": q}, device_id_type=MESH,
            ).wait_recv()

        each(pool - 1, got)
        lane = lax.broadcasted_iota(jnp.int32, (block, 128), 1)
        sub = lax.broadcasted_iota(jnp.int32, (block, 128), 0)

        def ids(q):
            row = meta[pl.ds(q * 8, 1), :]
            col = jnp.sum(jnp.where(lane == sub, row, 0), axis=1, keepdims=True)
            idcol[pl.ds(pl.multiple_of(q * block, block), block), :] = jnp.broadcast_to(
                col, (block, 128)
            )

        each(pool, ids)

        def quad(q):
            parts = [meta[pl.ds((q * 4 + s) * 8 + 1, 1), :] for s in range(4)]
            for half in range(2):
                line = jnp.concatenate([t[:, half * HALF : (half + 1) * HALF] for t in parts], axis=1)

                def part(t):
                    at = pl.ds(pl.multiple_of(t * tile, tile), tile)
                    row = lax.broadcasted_iota(jnp.int32, (tile, 128), 0) + t * tile
                    expand[half, at, pl.ds(pl.multiple_of(q * 128, 128), 128)] = jnp.where(
                        row == line, 1.0, 0.0
                    ).astype(BF16)

                each(rows // tile, part)

        each(pool // 4, quad)

    lax.fori_loop(0, CHUNKS + 2, step, 0)

    own_list = meta[pl.ds(me * 8 + 1, 1), :]
    eye = lax.broadcasted_iota(jnp.int32, (SLOTS, 128), 0) == lax.broadcasted_iota(
        jnp.int32, (SLOTS, 128), 1
    )
    own_col = jnp.sum(jnp.where(eye, own_list, 0), axis=1, keepdims=True)
    pick = jnp.where(
        own_col == lax.broadcasted_iota(jnp.int32, (SLOTS, rows), 1), 1.0, 0.0
    ).astype(BF16)
    low = jnp.dot(pick, accd[...].astype(BF16), preferred_element_type=F32)
    picked = jnp.dot(pick, idcol[...].astype(F32).astype(BF16), preferred_element_type=F32)
    slot = picked - (me * ADP_DEV).astype(F32)
    lane = lax.broadcasted_iota(jnp.int32, (SLOTS, 128), 1)
    low = jnp.where(slot == (lane // ADAPTER_RANK).astype(F32), low, 0.0)
    low = low[:, :ADAPTER_RANK] + low[:, ADAPTER_RANK:]
    mine_c = pl.ds(pl.multiple_of(me * HALF, HALF), HALF)
    comp[mine_c, :] = jnp.concatenate([low[:HALF], low[HALF:]], axis=1).astype(BF16)

    def share(i):
        return pltpu.make_async_remote_copy(
            src_ref=comp.at[mine_c, :],
            dst_ref=comp.at[mine_c, :],
            send_sem=c_send.at[i],
            recv_sem=c_recv.at[me],
            device_id={"pool": lax.rem(me + 1 + i, pool)},
            device_id_type=MESH,
        )

    each(pool - 1, lambda i: share(i).start())
    base(CHUNKS - 1)
    load_u.wait()

    def got(i):
        q = lax.rem(me + 1 + i, pool)
        at = pl.ds(pl.multiple_of(q * HALF, HALF), HALF)
        pltpu.make_async_remote_copy(
            src_ref=comp.at[at, :], dst_ref=comp.at[at, :], send_sem=c_send.at[0],
            recv_sem=c_recv.at[q], device_id={"pool": q}, device_id_type=MESH,
        ).wait_recv()

    each(pool - 1, got)

    def finish(t):
        at = pl.ds(pl.multiple_of(t * tile, tile), tile)
        first = jnp.dot(expand[0, at, :], comp[...], preferred_element_type=F32)
        second = jnp.dot(expand[1, at, :], comp[...], preferred_element_type=F32)
        factor = first[:, :ADAPTER_RANK] + second[:, ADAPTER_RANK:]
        pair = jnp.concatenate([factor, factor], axis=1).astype(BF16).astype(F32)
        ids = idcol[at, :] - lax.broadcasted_iota(jnp.int32, (tile, 128), 1) // ADAPTER_RANK

        def spread(q):
            wide[:, pl.ds(pl.multiple_of(q * 128, 128), 128)] = jnp.where(
                ids == q * ADP_DEV, pair, 0.0
            ).astype(BF16)

        bank = u.shape[0] // 128
        for q in range(bank):
            spread(q)
        delta = jnp.dot(wide[...], u[...], preferred_element_type=F32)
        out_ref[at, :] = (acc[at, :] + delta).astype(BF16)

    each(rows // tile, finish)

    def done(k):
        each(nz - 1, lambda i: to_z(k, i).wait_send())
        for i in range(ny - 1):
            each(nz, lambda zz: to_y(k, zz, i).wait_send())
        for yy in range(ny):
            each(nz, lambda zz: to_s(k, zz, yy).wait_send())

    lax.fori_loop(0, CHUNKS, lambda k, t: (done(k), t)[1], 0)
    each(pool - 1, lambda i: tell(i).wait_send())
    each(pool - 1, lambda i: share(i).wait_send())


def local(nz, ny, hidden, gain, weight, down, up, ids, requests):
    pool = nz * ny * 2
    block, width = hidden.shape
    rows = block * pool
    n = weight.shape[1]
    tile = min(rows, 256)
    dma = pltpu.SemaphoreType.DMA
    vm = pl.BlockSpec(memory_space=pltpu.VMEM)
    hbm = pl.BlockSpec(memory_space=pl.ANY)
    return pl.pallas_call(
        functools.partial(kernel, nz, ny),
        out_shape=jax.ShapeDtypeStruct((rows, n), BF16),
        in_specs=[hbm, vm, hbm, hbm, hbm, vm, vm],
        out_specs=vm,
        scratch_shapes=[
            pltpu.VMEM((rows, width), BF16),
            pltpu.VMEM(weight.shape, BF16),
            pltpu.VMEM(down.shape, BF16),
            pltpu.VMEM(up.shape, BF16),
            pltpu.VMEM((block, width), BF16),
            pltpu.VMEM((rows, n), F32),
            pltpu.VMEM((rows, down.shape[1]), F32),
            pltpu.VMEM((pool * 8, 128), jnp.int32),
            pltpu.VMEM((pool * HALF, 128), BF16),
            pltpu.VMEM((2, rows, pool * HALF), BF16),
            pltpu.VMEM((rows, 128), jnp.int32),
            pltpu.VMEM((tile, up.shape[0]), BF16),
            dma,
            dma((CHUNKS,)),
            dma((CHUNKS,)),
            dma,
            dma((CHUNKS, nz)),
            dma((CHUNKS, nz * max(ny - 1, 1))),
            dma((CHUNKS, nz * ny)),
            dma((CHUNKS, pool)),
            dma((pool,)),
            dma((pool,)),
            dma((pool,)),
            dma((pool,)),
        ],
        compiler_params=pltpu.CompilerParams(
            collective_id=0, has_side_effects=True, vmem_limit_bytes=56 * 1024 * 1024
        ),
    )(hidden, gain.reshape(1, -1), weight, down, up, ids, requests)


def solution(mesh):
    pool = mesh.shape["pool"]
    ny = 2 if pool == 16 else 1
    nz = pool // (2 * ny)
    return jax.shard_map(
        functools.partial(local, nz, ny),
        mesh=mesh,
        in_specs=(
            P(("groups", "pool"), None),
            P(),
            P(None, "pool"),
            P(None, ("groups", "pool")),
            P("groups", "pool"),
            P(("groups", "pool")),
            P(("groups", "pool")),
        ),
        out_specs=P("groups", "pool"),
        check_vma=False,
    )
```

```python
import functools

import jax
import jax.numpy as jnp
from jax import lax
from jax.experimental import pallas as pl
from jax.experimental.pallas import tpu as pltpu
from jax.sharding import PartitionSpec as P

ADAPTER_RANK = 64
ADP_DEV = 2
SLOTS = 64
HALF = SLOTS // 2
CHUNKS = 8
AHEAD = 3
AHEAD_Y = 3
LAG_Y = 2
LAG = 3
MESH = pl.DeviceIdType.MESH
F32, BF16 = jnp.float32, jnp.bfloat16


def each(n, body):
    if n <= 8:
        for i in range(n):
            body(i)
    else:

        def step(i, carry):
            body(i)
            return carry

        lax.fori_loop(0, n, step, 0)


def kernel(
    nz, ny, h_hbm, g_hbm, w_hbm, d_hbm, u_hbm, ids_ref, list_ref, out_ref,
    x, w, d, u, h, g, acc, accd, meta, comp, expand, idcol, wide,
    h_sem, g_sem, w_sem, d_sem, u_sem, z_send, y_send, s_send, recv, s_recv,
    m_send, m_recv, c_send, c_recv,
):
    pool = nz * ny * 2
    lines = nz * ny
    block, width = h_hbm.shape
    rows = block * pool
    kc = width // CHUNKS
    tile = min(rows, 256)
    me = lax.axis_index("pool")
    c = lax.rem(me, 2)
    y = lax.rem(me // 2, ny)
    z = me // (2 * ny)

    def pid(zz, yy, cc):
        return (zz * ny + yy) * 2 + cc

    def place(zz, yy, cc):
        return (cc * ny + yy) * nz + zz

    def row_of(b):
        at = b // block
        zz, yy, cc = lax.rem(at, nz), lax.rem(at // nz, ny), at // lines
        return pid(zz, yy, cc) * block + lax.rem(b, block)

    here = place(z, y, c)

    def to(sem, recv_sem, src, target):
        return pltpu.make_async_remote_copy(
            src_ref=src, dst_ref=src, send_sem=sem, recv_sem=recv_sem,
            device_id={"pool": target}, device_id_type=MESH,
        )

    load_h = pltpu.make_async_copy(h_hbm, h, h_sem)
    load_g = pltpu.make_async_copy(g_hbm, g, g_sem)
    load_h.start()
    load_g.start()

    barrier = pltpu.get_barrier_semaphore()

    def greet(q):
        pl.semaphore_signal(barrier, inc=1, device_id={"pool": q}, device_id_type=MESH)

    greet(pid(z, y, 1 - c))
    each(ny - 1, lambda i: greet(pid(z, lax.rem(y + 1 + i, ny), c)))
    each(nz - 1, lambda i: greet(pid(lax.rem(z + 1 + i, nz), y, c)))

    mine8 = pl.ds(pl.multiple_of(here * 8, 8), 8)
    meta[mine8, :] = jnp.full((8, 128), -1, jnp.int32)
    meta[pl.ds(here * 8, 1), pl.ds(0, block)] = ids_ref[...].reshape(1, block)
    entries = list_ref.shape[0]
    meta[pl.ds(here * 8 + 1, 1), pl.ds(0, entries)] = list_ref[...].reshape(1, entries)

    def cols(k):
        return pl.ds(pl.multiple_of(k * kc, kc), kc)

    def load_w(k):
        return pltpu.make_async_copy(w_hbm.at[cols(k), :], w.at[cols(k), :], w_sem.at[k])

    def load_d(k):
        return pltpu.make_async_copy(d_hbm.at[cols(k), :], d.at[cols(k), :], d_sem.at[k])

    load_u = pltpu.make_async_copy(u_hbm, u, u_sem)

    load_h.wait()
    load_g.wait()
    for k in range(CHUNKS):
        load_d(k).start()
        load_w(k).start()
    load_u.start()

    total = jnp.zeros((block, 128), F32)
    for k in range(CHUNKS):
        v = h[:, k * kc : (k + 1) * kc].astype(F32)
        v = v * v
        for j in range(kc // 128):
            total = total + v[:, j * 128 : (j + 1) * 128]
    mean = jnp.sum(total, axis=1, keepdims=True) / width
    scale = lax.rsqrt(mean + 1e-05)
    mine = pl.ds(pl.multiple_of(here * block, block), block)
    for k in range(CHUNKS):
        v = h[:, k * kc : (k + 1) * kc].astype(F32)
        gain = g[k * kc : (k + 1) * kc].astype(F32).reshape(1, kc)
        x[mine, k * kc : (k + 1) * kc] = (v * scale * gain).astype(BF16)

    pl.semaphore_wait(barrier, nz + ny - 1)

    def piece(at, k, count=1):
        size = block * count
        return x.at[pl.ds(pl.multiple_of(at * block, size), size), cols(k)]

    near = nz == 4

    def far(zz):
        return (zz - z == 3) | (z - zz == 3)

    def to_z(k, i):
        zz = lax.rem(z + 1 + i, nz)
        return to(z_send.at[k, i], recv.at[k, here], piece(here, k), pid(zz, y, c))

    def z_sends(k, act):
        def one(i):
            if near:

                @pl.when(jnp.logical_not(far(lax.rem(z + 1 + i, nz))))
                def _():
                    act(to_z(k, i))
            else:
                act(to_z(k, i))

        each(nz - 1, one)

    def relay(k, act):
        @pl.when((z == 1) | (z == 2))
        def _():
            at = place(6 - 3 * z, y, c)
            act(to(z_send.at[k, nz - 1], recv.at[k, at], piece(at, k), pid(3 * z - 3, y, c)))

    def to_y(k, zz, i):
        at = place(zz, y, c)
        yy = lax.rem(y + 1 + i, ny)
        return to(y_send.at[k, zz * max(ny - 1, 1) + i], recv.at[k, at], piece(at, k), pid(z, yy, c))

    def to_s(k, yy):
        at = place(0, yy, c)
        return to(s_send.at[k, yy], s_recv.at[k, yy], piece(at, k, nz), pid(z, y, 1 - c))

    def arrived(k, at):
        to(z_send.at[0, 0], recv.at[k, at], piece(at, k), pid(z, y, 1 - c)).wait_recv()

    def from_s(k, yy):
        at = place(0, yy, 1 - c)
        to(s_send.at[0, 0], s_recv.at[k, yy], piece(at, k, nz), pid(z, y, 1 - c)).wait_recv()

    def own_y(k):
        each(ny - 1, lambda i: to_y(k, z, i).start())

    def own_z(k):
        z_sends(k, lambda t: t.start())

    for k in range(max(AHEAD, AHEAD_Y)):
        if k < AHEAD:
            own_z(k)
        if k < AHEAD_Y:
            own_y(k)

    acc[...] = jnp.zeros_like(acc)
    accd[...] = jnp.zeros_like(accd)

    def spread_to(buf, size, sem, recv_sem, i):
        q = lax.rem(here - c * lines + 1 + i, lines)
        at = pl.ds(pl.multiple_of(here * size, size), size)
        return to(
            sem.at[i], recv_sem.at[here], buf.at[at, :], pid(lax.rem(q, nz), q // nz, c)
        )

    def spread_from(buf, size, sem, recv_sem, i):
        q = c * lines + lax.rem(here - c * lines + 1 + i, lines)
        at = pl.ds(pl.multiple_of(q * size, size), size)
        to(sem.at[0], recv_sem.at[q], buf.at[at, :], pid(z, y, 1 - c)).wait_recv()

    def across(buf, size, sem, recv_sem, cc):
        at = pl.ds(pl.multiple_of(cc * lines * size, lines * size), lines * size)
        return to(sem.at[lines], recv_sem.at[pool], buf.at[at, :], pid(z, y, 1 - c))

    telling = (meta, 8, m_send, m_recv)
    sharing = (comp, HALF, c_send, c_recv)

    def down(k):
        load_d(k).wait()

        def part(t):
            at = pl.ds(pl.multiple_of(t * tile, tile), tile)
            accd[at, :] += jnp.dot(x[at, cols(k)], d[cols(k), :], preferred_element_type=F32)

        each(rows // tile, part)

    def base(k):
        load_w(k).wait()

        def part(t):
            at = pl.ds(pl.multiple_of(t * tile, tile), tile)
            acc[at, :] += jnp.dot(x[at, cols(k)], w[cols(k), :], preferred_element_type=F32)

        each(rows // tile, part)

    def step(i, carry):
        @pl.when(i + AHEAD < CHUNKS)
        def _():
            own_z(i + AHEAD)

        @pl.when(i + AHEAD_Y < CHUNKS)
        def _():
            own_y(i + AHEAD_Y)

        @pl.when(i < CHUNKS)
        def _():
            def from_z(j):
                zz = lax.rem(z + 1 + j, nz)
                arrived(i, place(zz, y, c))
                if near:

                    @pl.when(((z == 1) | (z == 2)) & (zz == 6 - 3 * z))
                    def _():
                        relay(i, lambda t: t.start())

                each(ny - 1, lambda t: to_y(i, zz, t).start())

            each(nz - 1, from_z)
            to_s(i, y).start()

        @pl.when((i >= LAG_Y) & (i < CHUNKS + LAG_Y))
        def _():
            def from_y(t):
                yy = lax.rem(y + 1 + t, ny)
                each(nz, lambda zz: arrived(i - LAG_Y, place(zz, yy, c)))
                to_s(i - LAG_Y, yy).start()

            each(ny - 1, from_y)

        @pl.when(i >= LAG)
        def _():
            each(ny, lambda yy: from_s(i - LAG, yy))

            @pl.when(i == LAG)
            def _():
                each(lines - 1, lambda t: spread_to(*telling, t).start())

            @pl.when(i == LAG + 2)
            def _():
                each(lines - 1, lambda t: spread_from(*telling, t))
                across(*telling, c).start()

            down(i - LAG)

            @pl.when(i - LAG < CHUNKS - 1)
            def _():
                base(i - LAG)

        @pl.when(i == LAG + 3)
        def _():
            tables()

        return carry

    def tables():
        across(*telling, 1 - c).wait_recv()
        lane = lax.broadcasted_iota(jnp.int32, (block, 128), 1)
        sub = lax.broadcasted_iota(jnp.int32, (block, 128), 0)

        def ids(q):
            row = meta[pl.ds(q * 8, 1), :]
            col = jnp.sum(jnp.where(lane == sub, row, 0), axis=1, keepdims=True)
            idcol[pl.ds(pl.multiple_of(q * block, block), block), :] = jnp.broadcast_to(
                col, (block, 128)
            )

        each(pool, ids)

        def part(t):
            at = pl.ds(pl.multiple_of(t * tile, tile), tile)
            row = row_of(lax.broadcasted_iota(jnp.int32, (tile, 128), 0) + t * tile)

            def quad(q):
                parts = [meta[pl.ds((q * 4 + s) * 8 + 1, 1), :] for s in range(4)]
                for half in range(2):
                    line = jnp.concatenate(
                        [t[:, half * HALF : (half + 1) * HALF] for t in parts], axis=1
                    )
                    expand[half, at, pl.ds(pl.multiple_of(q * 128, 128), 128)] = jnp.where(
                        row == line, 1.0, 0.0
                    ).astype(BF16)

            each(pool // 4, quad)

        each(rows // tile, part)

    lax.fori_loop(0, CHUNKS + LAG, step, 0)

    own_list = meta[pl.ds(here * 8 + 1, 1), :]
    eye = lax.broadcasted_iota(jnp.int32, (SLOTS, 128), 0) == lax.broadcasted_iota(
        jnp.int32, (SLOTS, 128), 1
    )
    own_col = jnp.sum(jnp.where(eye, own_list, 0), axis=1, keepdims=True)
    pick = jnp.where(
        own_col == row_of(lax.broadcasted_iota(jnp.int32, (SLOTS, rows), 1)), 1.0, 0.0
    ).astype(BF16)
    low = jnp.dot(pick, accd[...].astype(BF16), preferred_element_type=F32)
    picked = jnp.dot(pick, idcol[...].astype(F32).astype(BF16), preferred_element_type=F32)
    slot = picked - (me * ADP_DEV).astype(F32)
    lane = lax.broadcasted_iota(jnp.int32, (SLOTS, 128), 1)
    low = jnp.where(slot == (lane // ADAPTER_RANK).astype(F32), low, 0.0)
    low = low[:, :ADAPTER_RANK] + low[:, ADAPTER_RANK:]
    mine_c = pl.ds(pl.multiple_of(here * HALF, HALF), HALF)
    comp[mine_c, :] = jnp.concatenate([low[:HALF], low[HALF:]], axis=1).astype(BF16)

    each(lines - 1, lambda i: spread_to(*sharing, i).start())
    base(CHUNKS - 1)
    load_u.wait()
    each(lines - 1, lambda i: spread_from(*sharing, i))
    across(*sharing, c).start()
    across(*sharing, 1 - c).wait_recv()

    def finish(t):
        at = pl.ds(pl.multiple_of(t * tile, tile), tile)
        first = jnp.dot(expand[0, at, :], comp[...], preferred_element_type=F32)
        second = jnp.dot(expand[1, at, :], comp[...], preferred_element_type=F32)
        factor = first[:, :ADAPTER_RANK] + second[:, ADAPTER_RANK:]
        pair = jnp.concatenate([factor, factor], axis=1).astype(BF16).astype(F32)
        ids = idcol[at, :] - lax.broadcasted_iota(jnp.int32, (tile, 128), 1) // ADAPTER_RANK
        for q in range(u.shape[0] // 128):
            wide[:, q * 128 : (q + 1) * 128] = jnp.where(ids == q * ADP_DEV, pair, 0.0).astype(BF16)
        delta = jnp.dot(wide[...], u[...], preferred_element_type=F32)
        result = (acc[at, :] + delta).astype(BF16)
        for s in range(tile // block):
            row = row_of((t * (tile // block) + s) * block)
            out_ref[pl.ds(pl.multiple_of(row, block), block), :] = result[s * block : (s + 1) * block]

    each(rows // tile, finish)

    def done(k):
        z_sends(k, lambda t: t.wait_send())
        if near:
            relay(k, lambda t: t.wait_send())
        for i in range(ny - 1):
            each(nz, lambda zz: to_y(k, zz, i).wait_send())
        for yy in range(ny):
            to_s(k, yy).wait_send()

    lax.fori_loop(0, CHUNKS, lambda k, t: (done(k), t)[1], 0)
    for what in (telling, sharing):
        each(lines - 1, lambda i: spread_to(*what, i).wait_send())
        across(*what, c).wait_send()


def local(nz, ny, hidden, gain, weight, down, up, ids, requests):
    pool = nz * ny * 2
    block, width = hidden.shape
    rows = block * pool
    n = weight.shape[1]
    tile = min(rows, 256)
    dma = pltpu.SemaphoreType.DMA
    vm = pl.BlockSpec(memory_space=pltpu.VMEM)
    hbm = pl.BlockSpec(memory_space=pl.ANY)
    return pl.pallas_call(
        functools.partial(kernel, nz, ny),
        out_shape=jax.ShapeDtypeStruct((rows, n), BF16),
        in_specs=[hbm, hbm, hbm, hbm, hbm, vm, vm],
        out_specs=vm,
        scratch_shapes=[
            pltpu.VMEM((rows, width), BF16),
            pltpu.VMEM(weight.shape, BF16),
            pltpu.VMEM(down.shape, BF16),
            pltpu.VMEM(up.shape, BF16),
            pltpu.VMEM((block, width), BF16),
            pltpu.VMEM((width,), BF16),
            pltpu.VMEM((rows, n), F32),
            pltpu.VMEM((rows, down.shape[1]), F32),
            pltpu.VMEM((pool * 8, 128), jnp.int32),
            pltpu.VMEM((pool * HALF, 128), BF16),
            pltpu.VMEM((2, rows, pool * HALF), BF16),
            pltpu.VMEM((rows, 128), jnp.int32),
            pltpu.VMEM((tile, up.shape[0]), BF16),
            dma,
            dma,
            dma((CHUNKS,)),
            dma((CHUNKS,)),
            dma,
            dma((CHUNKS, nz)),
            dma((CHUNKS, nz * max(ny - 1, 1))),
            dma((CHUNKS, ny)),
            dma((CHUNKS, pool)),
            dma((CHUNKS, ny)),
            dma((pool,)),
            dma((pool + 1,)),
            dma((pool,)),
            dma((pool + 1,)),
        ],
        compiler_params=pltpu.CompilerParams(
            collective_id=0, has_side_effects=True, vmem_limit_bytes=56 * 1024 * 1024
        ),
    )(hidden, gain, weight, down, up, ids, requests)


def solution(mesh):
    pool = mesh.shape["pool"]
    ny = 2 if pool == 16 else 1
    nz = pool // (2 * ny)
    return jax.shard_map(
        functools.partial(local, nz, ny),
        mesh=mesh,
        in_specs=(
            P(("groups", "pool"), None),
            P(),
            P(None, "pool"),
            P(None, ("groups", "pool")),
            P("groups", "pool"),
            P(("groups", "pool")),
            P(("groups", "pool")),
        ),
        out_specs=P("groups", "pool"),
        check_vma=False,
    )
```

```python
import functools

import jax
import jax.numpy as jnp
from jax import lax
from jax.experimental import pallas as pl
from jax.experimental.pallas import tpu as pltpu
from jax.sharding import PartitionSpec as P

ADAPTER_RANK = 64
ADP_DEV = 2
SLOTS = 64
HALF = SLOTS // 2
CHUNKS = 8
AHEAD = 3
AHEAD_Y = 3
LAG_Y = 2
LAG = 3
MESH = pl.DeviceIdType.MESH
F32, BF16 = jnp.float32, jnp.bfloat16


DEFER = 3


def each(n, body):
    if n <= 8:
        for i in range(n):
            body(i)
    else:

        def step(i, carry):
            body(i)
            return carry

        lax.fori_loop(0, n, step, 0)


def kernel(
    nz, ny, h_hbm, g_hbm, w_hbm, d_hbm, u_hbm, ids_ref, list_ref, out_ref,
    x, w, d, u, h, g, acc, accd, meta, comp, expand, idcol, wide,
    h_sem, g_sem, w_sem, d_sem, u_sem, z_send, p_send, y_send, s_send, recv, s_recv,
    m_send, m_recv, c_send, c_recv,
):
    pool = nz * ny * 2
    lines = nz * ny
    block, width = h_hbm.shape
    rows = block * pool
    kc = width // CHUNKS
    tile = min(rows, 256)
    me = lax.axis_index("pool")
    c = lax.rem(me, 2)
    y = lax.rem(me // 2, ny)
    z = me // (2 * ny)

    def pid(zz, yy, cc):
        return (zz * ny + yy) * 2 + cc

    def place(zz, yy, cc):
        return (cc * ny + yy) * nz + zz

    def row_of(b):
        at = b // block
        zz, yy, cc = lax.rem(at, nz), lax.rem(at // nz, ny), at // lines
        return pid(zz, yy, cc) * block + lax.rem(b, block)

    here = place(z, y, c)

    def to(sem, recv_sem, src, target):
        return pltpu.make_async_remote_copy(
            src_ref=src, dst_ref=src, send_sem=sem, recv_sem=recv_sem,
            device_id={"pool": target}, device_id_type=MESH,
        )

    load_h = pltpu.make_async_copy(h_hbm, h, h_sem)
    load_g = pltpu.make_async_copy(g_hbm, g, g_sem)
    load_h.start()
    load_g.start()

    barrier = pltpu.get_barrier_semaphore()

    def greet(q):
        pl.semaphore_signal(barrier, inc=1, device_id={"pool": q}, device_id_type=MESH)

    greet(pid(z, y, 1 - c))
    each(ny - 1, lambda i: greet(pid(z, lax.rem(y + 1 + i, ny), c)))
    each(nz - 1, lambda i: greet(pid(lax.rem(z + 1 + i, nz), y, c)))

    mine8 = pl.ds(pl.multiple_of(here * 8, 8), 8)
    meta[mine8, :] = jnp.full((8, 128), -1, jnp.int32)
    meta[pl.ds(here * 8, 1), pl.ds(0, block)] = ids_ref[...].reshape(1, block)
    entries = list_ref.shape[0]
    meta[pl.ds(here * 8 + 1, 1), pl.ds(0, entries)] = list_ref[...].reshape(1, entries)

    def cols(k):
        return pl.ds(pl.multiple_of(k * kc, kc), kc)

    def load_w(k):
        return pltpu.make_async_copy(w_hbm.at[cols(k), :], w.at[cols(k), :], w_sem.at[k])

    def load_d(k):
        return pltpu.make_async_copy(d_hbm.at[cols(k), :], d.at[cols(k), :], d_sem.at[k])

    load_u = pltpu.make_async_copy(u_hbm, u, u_sem)

    load_h.wait()
    load_g.wait()
    for k in range(CHUNKS):
        load_d(k).start()
        load_w(k).start()
    load_u.start()

    total = jnp.zeros((block, 128), F32)
    for k in range(CHUNKS):
        v = h[:, k * kc : (k + 1) * kc].astype(F32)
        v = v * v
        for j in range(kc // 128):
            total = total + v[:, j * 128 : (j + 1) * 128]
    mean = jnp.sum(total, axis=1, keepdims=True) / width
    scale = lax.rsqrt(mean + 1e-05)
    mine = pl.ds(pl.multiple_of(here * block, block), block)
    for k in range(CHUNKS):
        v = h[:, k * kc : (k + 1) * kc].astype(F32)
        gain = g[k * kc : (k + 1) * kc].astype(F32).reshape(1, kc)
        x[mine, k * kc : (k + 1) * kc] = (v * scale * gain).astype(BF16)

    pl.semaphore_wait(barrier, nz + ny - 1)

    def piece(at, k, count=1):
        size = block * count
        return x.at[pl.ds(pl.multiple_of(at * block, size), size), cols(k)]

    near = nz == 4

    def far(zz):
        return (zz - z == 3) | (z - zz == 3)

    def to_z(k, i):
        zz = lax.rem(z + 1 + i, nz)
        return to(z_send.at[k, i], recv.at[k, here], piece(here, k), pid(zz, y, c))

    def to_z_peer(k, i):
        at = place(z, lax.rem(y + 1, ny), c)
        zz = lax.rem(z + 1 + i, nz)
        return to(p_send.at[i], recv.at[k, at], piece(at, k), pid(zz, y, c))

    def z_sends(k, act, to_z=to_z):
        def one(i):
            if near:

                @pl.when(jnp.logical_not(far(lax.rem(z + 1 + i, nz))))
                def _():
                    act(to_z(k, i))
            else:
                act(to_z(k, i))

        each(nz - 1, one)

    def relay(k, act, yy, sem):
        at = place(6 - 3 * z, yy, c)
        act(to(sem, recv.at[k, at], piece(at, k), pid(3 * z - 3, y, c)))

    middle = (z == 1) | (z == 2)
    both = ny == 2
    last = CHUNKS - 1
    regular = CHUNKS - 1 if both else CHUNKS
    peer = lax.rem(y + 1, ny)

    def to_y(k, zz, i):
        at = place(zz, y, c)
        yy = lax.rem(y + 1 + i, ny)
        return to(y_send.at[k, zz * max(ny - 1, 1) + i], recv.at[k, at], piece(at, k), pid(z, yy, c))

    def to_s(k, yy):
        at = place(0, yy, c)
        return to(s_send.at[k, yy], s_recv.at[k, yy], piece(at, k, nz), pid(z, y, 1 - c))

    def arrived(k, at):
        to(z_send.at[0, 0], recv.at[k, at], piece(at, k), pid(z, y, 1 - c)).wait_recv()

    def from_s(k, yy):
        at = place(0, yy, 1 - c)
        to(s_send.at[0, 0], s_recv.at[k, yy], piece(at, k, nz), pid(z, y, 1 - c)).wait_recv()

    def own_y(k):
        each(ny - 1, lambda i: to_y(k, z, i).start())

    def own_z(k):
        z_sends(k, lambda t: t.start())

    for k in range(max(AHEAD, AHEAD_Y)):
        if k < AHEAD:
            own_z(k)
        if k < AHEAD_Y:
            own_y(k)
    if both:
        own_y(last)

    acc[...] = jnp.zeros_like(acc)
    accd[...] = jnp.zeros_like(accd)

    def spread_to(buf, size, sem, recv_sem, i):
        q = lax.rem(here - c * lines + 1 + i, lines)
        at = pl.ds(pl.multiple_of(here * size, size), size)
        return to(
            sem.at[i], recv_sem.at[here], buf.at[at, :], pid(lax.rem(q, nz), q // nz, c)
        )

    def spread_from(buf, size, sem, recv_sem, i):
        q = c * lines + lax.rem(here - c * lines + 1 + i, lines)
        at = pl.ds(pl.multiple_of(q * size, size), size)
        to(sem.at[0], recv_sem.at[q], buf.at[at, :], pid(z, y, 1 - c)).wait_recv()

    def across(buf, size, sem, recv_sem, cc):
        at = pl.ds(pl.multiple_of(cc * lines * size, lines * size), lines * size)
        return to(sem.at[lines], recv_sem.at[pool], buf.at[at, :], pid(z, y, 1 - c))

    telling = (meta, 8, m_send, m_recv)
    sharing = (comp, HALF, c_send, c_recv)

    def down(k):
        load_d(k).wait()

        def part(t):
            at = pl.ds(pl.multiple_of(t * tile, tile), tile)
            accd[at, :] += jnp.dot(x[at, cols(k)], d[cols(k), :], preferred_element_type=F32)

        each(rows // tile, part)

    def base(k):
        load_w(k).wait()

        def part(t):
            at = pl.ds(pl.multiple_of(t * tile, tile), tile)
            acc[at, :] += jnp.dot(x[at, cols(k)], w[cols(k), :], preferred_element_type=F32)

        each(rows // tile, part)

    def step(i, carry):
        @pl.when(i + AHEAD < CHUNKS)
        def _():
            own_z(i + AHEAD)

        if both:

            @pl.when(i + AHEAD == last)
            def _():
                arrived(last, place(z, peer, c))
                z_sends(last, lambda t: t.start(), to_z_peer)

        @pl.when(i + AHEAD_Y < regular)
        def _():
            own_y(i + AHEAD_Y)

        @pl.when(i < regular)
        def _():
            def from_z(j):
                zz = lax.rem(z + 1 + j, nz)
                arrived(i, place(zz, y, c))
                if near:

                    @pl.when(middle & (zz == 6 - 3 * z))
                    def _():
                        relay(i, lambda t: t.start(), y, z_send.at[i, nz - 1])

                each(ny - 1, lambda t: to_y(i, zz, t).start())

            each(nz - 1, from_z)
            to_s(i, y).start()

        if both:

            @pl.when(i == last)
            def _():
                for yy, sem in ((y, z_send.at[last, nz - 1]), (peer, p_send.at[nz - 1])):

                    def from_z(j):
                        zz = lax.rem(z + 1 + j, nz)
                        arrived(last, place(zz, yy, c))
                        if near:

                            @pl.when(middle & (zz == 6 - 3 * z))
                            def _():
                                relay(last, lambda t: t.start(), yy, sem)

                    each(nz - 1, from_z)
                    to_s(last, yy).start()

        @pl.when((i >= LAG_Y) & (i < regular + LAG_Y))
        def _():
            def from_y(t):
                yy = lax.rem(y + 1 + t, ny)
                each(nz, lambda zz: arrived(i - LAG_Y, place(zz, yy, c)))
                to_s(i - LAG_Y, yy).start()

            each(ny - 1, from_y)

        @pl.when(i >= LAG)
        def _():
            each(ny, lambda yy: from_s(i - LAG, yy))

            @pl.when(i == LAG)
            def _():
                each(lines - 1, lambda t: spread_to(*telling, t).start())

            @pl.when(i == LAG + 2)
            def _():
                each(lines - 1, lambda t: spread_from(*telling, t))
                across(*telling, c).start()

            down(i - LAG)

            @pl.when(i - LAG < CHUNKS - DEFER)
            def _():
                base(i - LAG)

        @pl.when(i == LAG + 3)
        def _():
            tables()

        return carry

    def tables():
        across(*telling, 1 - c).wait_recv()
        lane = lax.broadcasted_iota(jnp.int32, (block, 128), 1)
        sub = lax.broadcasted_iota(jnp.int32, (block, 128), 0)

        def ids(q):
            row = meta[pl.ds(q * 8, 1), :]
            col = jnp.sum(jnp.where(lane == sub, row, 0), axis=1, keepdims=True)
            idcol[pl.ds(pl.multiple_of(q * block, block), block), :] = jnp.broadcast_to(
                col, (block, 128)
            )

        each(pool, ids)

    def one_hots():
        def part(t):
            at = pl.ds(pl.multiple_of(t * tile, tile), tile)
            row = row_of(lax.broadcasted_iota(jnp.int32, (tile, 128), 0) + t * tile)

            def quad(q):
                parts = [meta[pl.ds((q * 4 + s) * 8 + 1, 1), :] for s in range(4)]
                for half in range(2):
                    line = jnp.concatenate(
                        [t[:, half * HALF : (half + 1) * HALF] for t in parts], axis=1
                    )
                    expand[half, at, pl.ds(pl.multiple_of(q * 128, 128), 128)] = jnp.where(
                        row == line, 1.0, 0.0
                    ).astype(BF16)

            each(pool // 4, quad)

        each(rows // tile, part)

    lax.fori_loop(0, CHUNKS + LAG, step, 0)

    own_list = meta[pl.ds(here * 8 + 1, 1), :]
    eye = lax.broadcasted_iota(jnp.int32, (SLOTS, 128), 0) == lax.broadcasted_iota(
        jnp.int32, (SLOTS, 128), 1
    )
    own_col = jnp.sum(jnp.where(eye, own_list, 0), axis=1, keepdims=True)
    pick = jnp.where(
        own_col == row_of(lax.broadcasted_iota(jnp.int32, (SLOTS, rows), 1)), 1.0, 0.0
    ).astype(BF16)
    low = jnp.dot(pick, accd[...].astype(BF16), preferred_element_type=F32)
    picked = jnp.dot(pick, idcol[...].astype(F32).astype(BF16), preferred_element_type=F32)
    slot = picked - (me * ADP_DEV).astype(F32)
    lane = lax.broadcasted_iota(jnp.int32, (SLOTS, 128), 1)
    low = jnp.where(slot == (lane // ADAPTER_RANK).astype(F32), low, 0.0)
    low = low[:, :ADAPTER_RANK] + low[:, ADAPTER_RANK:]
    mine_c = pl.ds(pl.multiple_of(here * HALF, HALF), HALF)
    comp[mine_c, :] = jnp.concatenate([low[:HALF], low[HALF:]], axis=1).astype(BF16)

    each(lines - 1, lambda i: spread_to(*sharing, i).start())
    lax.fori_loop(CHUNKS - DEFER, CHUNKS, lambda k, t: (base(k), t)[1], 0)
    one_hots()
    load_u.wait()
    each(lines - 1, lambda i: spread_from(*sharing, i))
    across(*sharing, c).start()
    across(*sharing, 1 - c).wait_recv()

    def finish(t):
        at = pl.ds(pl.multiple_of(t * tile, tile), tile)
        first = jnp.dot(expand[0, at, :], comp[...], preferred_element_type=F32)
        second = jnp.dot(expand[1, at, :], comp[...], preferred_element_type=F32)
        factor = first[:, :ADAPTER_RANK] + second[:, ADAPTER_RANK:]
        pair = jnp.concatenate([factor, factor], axis=1).astype(BF16).astype(F32)
        ids = idcol[at, :] - lax.broadcasted_iota(jnp.int32, (tile, 128), 1) // ADAPTER_RANK
        for q in range(u.shape[0] // 128):
            wide[:, q * 128 : (q + 1) * 128] = jnp.where(ids == q * ADP_DEV, pair, 0.0).astype(BF16)
        delta = jnp.dot(wide[...], u[...], preferred_element_type=F32)
        result = (acc[at, :] + delta).astype(BF16)
        for s in range(tile // block):
            row = row_of((t * (tile // block) + s) * block)
            out_ref[pl.ds(pl.multiple_of(row, block), block), :] = result[s * block : (s + 1) * block]

    each(rows // tile, finish)

    def done(k):
        z_sends(k, lambda t: t.wait_send())
        if near:

            @pl.when(middle)
            def _():
                relay(k, lambda t: t.wait_send(), y, z_send.at[k, nz - 1])

        @pl.when(k < regular)
        def _():
            for i in range(ny - 1):
                each(nz, lambda zz: to_y(k, zz, i).wait_send())

        for yy in range(ny):
            to_s(k, yy).wait_send()

    lax.fori_loop(0, CHUNKS, lambda k, t: (done(k), t)[1], 0)
    if both:
        each(ny - 1, lambda i: to_y(last, z, i).wait_send())
        z_sends(last, lambda t: t.wait_send(), to_z_peer)
        if near:

            @pl.when(middle)
            def _():
                relay(last, lambda t: t.wait_send(), peer, p_send.at[nz - 1])

    for what in (telling, sharing):
        each(lines - 1, lambda i: spread_to(*what, i).wait_send())
        across(*what, c).wait_send()


def local(nz, ny, hidden, gain, weight, down, up, ids, requests):
    pool = nz * ny * 2
    block, width = hidden.shape
    rows = block * pool
    n = weight.shape[1]
    tile = min(rows, 256)
    dma = pltpu.SemaphoreType.DMA
    vm = pl.BlockSpec(memory_space=pltpu.VMEM)
    hbm = pl.BlockSpec(memory_space=pl.ANY)
    return pl.pallas_call(
        functools.partial(kernel, nz, ny),
        out_shape=jax.ShapeDtypeStruct((rows, n), BF16),
        in_specs=[hbm, hbm, hbm, hbm, hbm, vm, vm],
        out_specs=vm,
        scratch_shapes=[
            pltpu.VMEM((rows, width), BF16),
            pltpu.VMEM(weight.shape, BF16),
            pltpu.VMEM(down.shape, BF16),
            pltpu.VMEM(up.shape, BF16),
            pltpu.VMEM((block, width), BF16),
            pltpu.VMEM((width,), BF16),
            pltpu.VMEM((rows, n), F32),
            pltpu.VMEM((rows, down.shape[1]), F32),
            pltpu.VMEM((pool * 8, 128), jnp.int32),
            pltpu.VMEM((pool * HALF, 128), BF16),
            pltpu.VMEM((2, rows, pool * HALF), BF16),
            pltpu.VMEM((rows, 128), jnp.int32),
            pltpu.VMEM((tile, up.shape[0]), BF16),
            dma,
            dma,
            dma((CHUNKS,)),
            dma((CHUNKS,)),
            dma,
            dma((CHUNKS, nz)),
            dma((nz,)),
            dma((CHUNKS, nz * max(ny - 1, 1))),
            dma((CHUNKS, ny)),
            dma((CHUNKS, pool)),
            dma((CHUNKS, ny)),
            dma((pool,)),
            dma((pool + 1,)),
            dma((pool,)),
            dma((pool + 1,)),
        ],
        compiler_params=pltpu.CompilerParams(
            collective_id=0, has_side_effects=True, vmem_limit_bytes=56 * 1024 * 1024
        ),
    )(hidden, gain, weight, down, up, ids, requests)


def solution(mesh):
    pool = mesh.shape["pool"]
    ny = 2 if pool == 16 else 1
    nz = pool // (2 * ny)
    return jax.shard_map(
        functools.partial(local, nz, ny),
        mesh=mesh,
        in_specs=(
            P(("groups", "pool"), None),
            P(),
            P(None, "pool"),
            P(None, ("groups", "pool")),
            P("groups", "pool"),
            P(("groups", "pool")),
            P(("groups", "pool")),
        ),
        out_specs=P("groups", "pool"),
        check_vma=False,
    )
```

```python
import functools

import jax
import jax.numpy as jnp
from jax import lax
from jax.experimental import pallas as pl
from jax.experimental.pallas import tpu as pltpu
from jax.sharding import PartitionSpec as P

ADAPTER_RANK = 64
ADP_DEV = 2
SLOTS = 64
HALF = SLOTS // 2
CHUNKS = 8
AHEAD = 3
AHEAD_Y = 3
LAG_Y = 2
LAG = 3
MESH = pl.DeviceIdType.MESH
F32, BF16 = jnp.float32, jnp.bfloat16


DEFER = 3


def each(n, body):
    if n <= 8:
        for i in range(n):
            body(i)
    else:

        def step(i, carry):
            body(i)
            return carry

        lax.fori_loop(0, n, step, 0)


def kernel(
    nz, ny, h_hbm, g_hbm, w_hbm, d_hbm, u_hbm, ids_ref, list_ref, out_ref,
    x, w, d, u, h, g, acc, accd, meta, comp, expand, idcol, wide,
    h_sem, g_sem, w_sem, d_sem, u_sem, z_send, p_send, y_send, s_send, recv, s_recv,
    m_send, m_recv, c_send, c_recv,
):
    pool = nz * ny * 2
    lines = nz * ny
    block, width = h_hbm.shape
    rows = block * pool
    kc = width // CHUNKS
    tile = min(rows, 256)
    me = lax.axis_index("pool")
    c = lax.rem(me, 2)
    y = lax.rem(me // 2, ny)
    z = me // (2 * ny)

    def pid(zz, yy, cc):
        return (zz * ny + yy) * 2 + cc

    def place(zz, yy, cc):
        return (cc * ny + yy) * nz + zz

    def row_of(b):
        at = b // block
        zz, yy, cc = lax.rem(at, nz), lax.rem(at // nz, ny), at // lines
        return pid(zz, yy, cc) * block + lax.rem(b, block)

    here = place(z, y, c)

    def to(sem, recv_sem, src, target):
        return pltpu.make_async_remote_copy(
            src_ref=src, dst_ref=src, send_sem=sem, recv_sem=recv_sem,
            device_id={"pool": target}, device_id_type=MESH,
        )

    load_h = pltpu.make_async_copy(h_hbm, h, h_sem)
    load_g = pltpu.make_async_copy(g_hbm, g, g_sem)
    load_h.start()
    load_g.start()

    barrier = pltpu.get_barrier_semaphore()

    def greet(q):
        pl.semaphore_signal(barrier, inc=1, device_id={"pool": q}, device_id_type=MESH)

    greet(pid(z, y, 1 - c))
    each(ny - 1, lambda i: greet(pid(z, lax.rem(y + 1 + i, ny), c)))
    each(nz - 1, lambda i: greet(pid(lax.rem(z + 1 + i, nz), y, c)))

    mine8 = pl.ds(pl.multiple_of(here * 8, 8), 8)
    meta[mine8, :] = jnp.full((8, 128), -1, jnp.int32)
    meta[pl.ds(here * 8, 1), pl.ds(0, block)] = ids_ref[...].reshape(1, block)
    entries = list_ref.shape[0]
    meta[pl.ds(here * 8 + 1, 1), pl.ds(0, entries)] = list_ref[...].reshape(1, entries)

    def cols(k):
        return pl.ds(pl.multiple_of(k * kc, kc), kc)

    def load_w(k):
        return pltpu.make_async_copy(w_hbm.at[cols(k), :], w.at[cols(k), :], w_sem.at[k])

    def load_d(k):
        return pltpu.make_async_copy(d_hbm.at[cols(k), :], d.at[cols(k), :], d_sem.at[k])

    load_u = pltpu.make_async_copy(u_hbm, u, u_sem)

    load_h.wait()
    load_g.wait()
    total = jnp.zeros((block, 128), F32)
    for k in range(CHUNKS):
        v = h[:, k * kc : (k + 1) * kc].astype(F32)
        v = v * v
        for j in range(kc // 128):
            total = total + v[:, j * 128 : (j + 1) * 128]
    mean = jnp.sum(total, axis=1, keepdims=True) / width
    scale = lax.rsqrt(mean + 1e-05)
    mine = pl.ds(pl.multiple_of(here * block, block), block)
    for k in range(CHUNKS):
        v = h[:, k * kc : (k + 1) * kc].astype(F32)
        gain = g[k * kc : (k + 1) * kc].astype(F32).reshape(1, kc)
        x[mine, k * kc : (k + 1) * kc] = (v * scale * gain).astype(BF16)

    pl.semaphore_wait(barrier, nz + ny - 1)

    def piece(at, k, count=1):
        size = block * count
        return x.at[pl.ds(pl.multiple_of(at * block, size), size), cols(k)]

    near = nz == 4

    def far(zz):
        return (zz - z == 3) | (z - zz == 3)

    def to_z(k, i):
        zz = lax.rem(z + 1 + i, nz)
        return to(z_send.at[k, i], recv.at[k, here], piece(here, k), pid(zz, y, c))

    def to_z_peer(k, i):
        at = place(z, lax.rem(y + 1, ny), c)
        zz = lax.rem(z + 1 + i, nz)
        return to(p_send.at[i], recv.at[k, at], piece(at, k), pid(zz, y, c))

    def z_sends(k, act, to_z=to_z):
        def one(i):
            if near:

                @pl.when(jnp.logical_not(far(lax.rem(z + 1 + i, nz))))
                def _():
                    act(to_z(k, i))
            else:
                act(to_z(k, i))

        each(nz - 1, one)

    def relay(k, act, yy, sem):
        at = place(6 - 3 * z, yy, c)
        act(to(sem, recv.at[k, at], piece(at, k), pid(3 * z - 3, y, c)))

    middle = (z == 1) | (z == 2)
    both = ny == 2
    last = CHUNKS - 1
    regular = CHUNKS - 1 if both else CHUNKS
    peer = lax.rem(y + 1, ny)

    def to_y(k, zz, i):
        at = place(zz, y, c)
        yy = lax.rem(y + 1 + i, ny)
        return to(y_send.at[k, zz * max(ny - 1, 1) + i], recv.at[k, at], piece(at, k), pid(z, yy, c))

    def to_s(k, yy):
        at = place(0, yy, c)
        return to(s_send.at[k, yy], s_recv.at[k, yy], piece(at, k, nz), pid(z, y, 1 - c))

    def arrived(k, at):
        to(z_send.at[0, 0], recv.at[k, at], piece(at, k), pid(z, y, 1 - c)).wait_recv()

    def from_s(k, yy):
        at = place(0, yy, 1 - c)
        to(s_send.at[0, 0], s_recv.at[k, yy], piece(at, k, nz), pid(z, y, 1 - c)).wait_recv()

    def own_y(k):
        each(ny - 1, lambda i: to_y(k, z, i).start())

    def own_z(k):
        z_sends(k, lambda t: t.start())

    for k in range(max(AHEAD, AHEAD_Y)):
        if k < AHEAD:
            own_z(k)
        if k < AHEAD_Y:
            own_y(k)
    if both:
        own_y(last)

    for k in range(CHUNKS):
        load_d(k).start()
        load_w(k).start()
    load_u.start()

    acc[...] = jnp.zeros_like(acc)
    accd[...] = jnp.zeros_like(accd)

    def spread_to(buf, size, sem, recv_sem, i):
        q = lax.rem(here - c * lines + 1 + i, lines)
        at = pl.ds(pl.multiple_of(here * size, size), size)
        return to(
            sem.at[i], recv_sem.at[here], buf.at[at, :], pid(lax.rem(q, nz), q // nz, c)
        )

    def spread_from(buf, size, sem, recv_sem, i):
        q = c * lines + lax.rem(here - c * lines + 1 + i, lines)
        at = pl.ds(pl.multiple_of(q * size, size), size)
        to(sem.at[0], recv_sem.at[q], buf.at[at, :], pid(z, y, 1 - c)).wait_recv()

    def across(buf, size, sem, recv_sem, cc):
        at = pl.ds(pl.multiple_of(cc * lines * size, lines * size), lines * size)
        return to(sem.at[lines], recv_sem.at[pool], buf.at[at, :], pid(z, y, 1 - c))

    telling = (meta, 8, m_send, m_recv)
    sharing = (comp, HALF, c_send, c_recv)

    def down(k):
        load_d(k).wait()

        def part(t):
            at = pl.ds(pl.multiple_of(t * tile, tile), tile)
            accd[at, :] += jnp.dot(x[at, cols(k)], d[cols(k), :], preferred_element_type=F32)

        each(rows // tile, part)

    def base(k):
        load_w(k).wait()

        def part(t):
            at = pl.ds(pl.multiple_of(t * tile, tile), tile)
            acc[at, :] += jnp.dot(x[at, cols(k)], w[cols(k), :], preferred_element_type=F32)

        each(rows // tile, part)

    def step(i, carry):
        @pl.when(i + AHEAD < CHUNKS)
        def _():
            own_z(i + AHEAD)

        if both:

            @pl.when(i + AHEAD == last)
            def _():
                arrived(last, place(z, peer, c))
                z_sends(last, lambda t: t.start(), to_z_peer)

        @pl.when(i + AHEAD_Y < regular)
        def _():
            own_y(i + AHEAD_Y)

        @pl.when(i < regular)
        def _():
            def from_z(j):
                zz = lax.rem(z + 1 + j, nz)
                arrived(i, place(zz, y, c))
                if near:

                    @pl.when(middle & (zz == 6 - 3 * z))
                    def _():
                        relay(i, lambda t: t.start(), y, z_send.at[i, nz - 1])

                each(ny - 1, lambda t: to_y(i, zz, t).start())

            each(nz - 1, from_z)
            to_s(i, y).start()

        if both:

            @pl.when(i == last)
            def _():
                for yy, sem in ((y, z_send.at[last, nz - 1]), (peer, p_send.at[nz - 1])):

                    def from_z(j):
                        zz = lax.rem(z + 1 + j, nz)
                        arrived(last, place(zz, yy, c))
                        if near:

                            @pl.when(middle & (zz == 6 - 3 * z))
                            def _():
                                relay(last, lambda t: t.start(), yy, sem)

                    each(nz - 1, from_z)
                    to_s(last, yy).start()

        @pl.when((i >= LAG_Y) & (i < regular + LAG_Y))
        def _():
            def from_y(t):
                yy = lax.rem(y + 1 + t, ny)
                each(nz, lambda zz: arrived(i - LAG_Y, place(zz, yy, c)))
                to_s(i - LAG_Y, yy).start()

            each(ny - 1, from_y)

        @pl.when(i >= LAG)
        def _():
            each(ny, lambda yy: from_s(i - LAG, yy))

            @pl.when(i == LAG)
            def _():
                each(lines - 1, lambda t: spread_to(*telling, t).start())

            @pl.when(i == LAG + 2)
            def _():
                each(lines - 1, lambda t: spread_from(*telling, t))
                across(*telling, c).start()

            down(i - LAG)

            @pl.when(i - LAG < CHUNKS - DEFER)
            def _():
                base(i - LAG)

        @pl.when(i == LAG + 3)
        def _():
            tables()

        return carry

    def tables():
        across(*telling, 1 - c).wait_recv()
        lane = lax.broadcasted_iota(jnp.int32, (block, 128), 1)
        sub = lax.broadcasted_iota(jnp.int32, (block, 128), 0)

        def ids(q):
            row = meta[pl.ds(q * 8, 1), :]
            col = jnp.sum(jnp.where(lane == sub, row, 0), axis=1, keepdims=True)
            idcol[pl.ds(pl.multiple_of(q * block, block), block), :] = jnp.broadcast_to(
                col, (block, 128)
            )

        each(pool, ids)

    def one_hots():
        def part(t):
            at = pl.ds(pl.multiple_of(t * tile, tile), tile)
            row = row_of(lax.broadcasted_iota(jnp.int32, (tile, 128), 0) + t * tile)

            def quad(q):
                parts = [meta[pl.ds((q * 4 + s) * 8 + 1, 1), :] for s in range(4)]
                for half in range(2):
                    line = jnp.concatenate(
                        [t[:, half * HALF : (half + 1) * HALF] for t in parts], axis=1
                    )
                    expand[half, at, pl.ds(pl.multiple_of(q * 128, 128), 128)] = jnp.where(
                        row == line, 1.0, 0.0
                    ).astype(BF16)

            each(pool // 4, quad)

        each(rows // tile, part)

    lax.fori_loop(0, CHUNKS + LAG, step, 0)

    own_list = meta[pl.ds(here * 8 + 1, 1), :]
    eye = lax.broadcasted_iota(jnp.int32, (SLOTS, 128), 0) == lax.broadcasted_iota(
        jnp.int32, (SLOTS, 128), 1
    )
    own_col = jnp.sum(jnp.where(eye, own_list, 0), axis=1, keepdims=True)
    pick = jnp.where(
        own_col == row_of(lax.broadcasted_iota(jnp.int32, (SLOTS, rows), 1)), 1.0, 0.0
    ).astype(BF16)
    low = jnp.dot(pick, accd[...].astype(BF16), preferred_element_type=F32)
    picked = jnp.dot(pick, idcol[...].astype(F32).astype(BF16), preferred_element_type=F32)
    slot = picked - (me * ADP_DEV).astype(F32)
    lane = lax.broadcasted_iota(jnp.int32, (SLOTS, 128), 1)
    low = jnp.where(slot == (lane // ADAPTER_RANK).astype(F32), low, 0.0)
    low = low[:, :ADAPTER_RANK] + low[:, ADAPTER_RANK:]
    mine_c = pl.ds(pl.multiple_of(here * HALF, HALF), HALF)
    comp[mine_c, :] = jnp.concatenate([low[:HALF], low[HALF:]], axis=1).astype(BF16)

    each(lines - 1, lambda i: spread_to(*sharing, i).start())
    lax.fori_loop(CHUNKS - DEFER, CHUNKS, lambda k, t: (base(k), t)[1], 0)
    one_hots()
    load_u.wait()
    each(lines - 1, lambda i: spread_from(*sharing, i))
    across(*sharing, c).start()
    across(*sharing, 1 - c).wait_recv()

    def finish(t):
        at = pl.ds(pl.multiple_of(t * tile, tile), tile)
        first = jnp.dot(expand[0, at, :], comp[...], preferred_element_type=F32)
        second = jnp.dot(expand[1, at, :], comp[...], preferred_element_type=F32)
        factor = first[:, :ADAPTER_RANK] + second[:, ADAPTER_RANK:]
        pair = jnp.concatenate([factor, factor], axis=1).astype(BF16).astype(F32)
        ids = idcol[at, :] - lax.broadcasted_iota(jnp.int32, (tile, 128), 1) // ADAPTER_RANK
        for q in range(u.shape[0] // 128):
            wide[:, q * 128 : (q + 1) * 128] = jnp.where(ids == q * ADP_DEV, pair, 0.0).astype(BF16)
        delta = jnp.dot(wide[...], u[...], preferred_element_type=F32)
        result = (acc[at, :] + delta).astype(BF16)
        for s in range(tile // block):
            row = row_of((t * (tile // block) + s) * block)
            out_ref[pl.ds(pl.multiple_of(row, block), block), :] = result[s * block : (s + 1) * block]

    each(rows // tile, finish)

    def done(k):
        z_sends(k, lambda t: t.wait_send())
        if near:

            @pl.when(middle)
            def _():
                relay(k, lambda t: t.wait_send(), y, z_send.at[k, nz - 1])

        @pl.when(k < regular)
        def _():
            for i in range(ny - 1):
                each(nz, lambda zz: to_y(k, zz, i).wait_send())

        for yy in range(ny):
            to_s(k, yy).wait_send()

    lax.fori_loop(0, CHUNKS, lambda k, t: (done(k), t)[1], 0)
    if both:
        each(ny - 1, lambda i: to_y(last, z, i).wait_send())
        z_sends(last, lambda t: t.wait_send(), to_z_peer)
        if near:

            @pl.when(middle)
            def _():
                relay(last, lambda t: t.wait_send(), peer, p_send.at[nz - 1])

    for what in (telling, sharing):
        each(lines - 1, lambda i: spread_to(*what, i).wait_send())
        across(*what, c).wait_send()


def local(nz, ny, hidden, gain, weight, down, up, ids, requests):
    pool = nz * ny * 2
    block, width = hidden.shape
    rows = block * pool
    n = weight.shape[1]
    tile = min(rows, 256)
    dma = pltpu.SemaphoreType.DMA
    vm = pl.BlockSpec(memory_space=pltpu.VMEM)
    hbm = pl.BlockSpec(memory_space=pl.ANY)
    return pl.pallas_call(
        functools.partial(kernel, nz, ny),
        out_shape=jax.ShapeDtypeStruct((rows, n), BF16),
        in_specs=[hbm, hbm, hbm, hbm, hbm, vm, vm],
        out_specs=vm,
        scratch_shapes=[
            pltpu.VMEM((rows, width), BF16),
            pltpu.VMEM(weight.shape, BF16),
            pltpu.VMEM(down.shape, BF16),
            pltpu.VMEM(up.shape, BF16),
            pltpu.VMEM((block, width), BF16),
            pltpu.VMEM((width,), BF16),
            pltpu.VMEM((rows, n), F32),
            pltpu.VMEM((rows, down.shape[1]), F32),
            pltpu.VMEM((pool * 8, 128), jnp.int32),
            pltpu.VMEM((pool * HALF, 128), BF16),
            pltpu.VMEM((2, rows, pool * HALF), BF16),
            pltpu.VMEM((rows, 128), jnp.int32),
            pltpu.VMEM((tile, up.shape[0]), BF16),
            dma,
            dma,
            dma((CHUNKS,)),
            dma((CHUNKS,)),
            dma,
            dma((CHUNKS, nz)),
            dma((nz,)),
            dma((CHUNKS, nz * max(ny - 1, 1))),
            dma((CHUNKS, ny)),
            dma((CHUNKS, pool)),
            dma((CHUNKS, ny)),
            dma((pool,)),
            dma((pool + 1,)),
            dma((pool,)),
            dma((pool + 1,)),
        ],
        compiler_params=pltpu.CompilerParams(
            collective_id=0, has_side_effects=True, vmem_limit_bytes=56 * 1024 * 1024
        ),
    )(hidden, gain, weight, down, up, ids, requests)


def solution(mesh):
    pool = mesh.shape["pool"]
    ny = 2 if pool == 16 else 1
    nz = pool // (2 * ny)
    return jax.shard_map(
        functools.partial(local, nz, ny),
        mesh=mesh,
        in_specs=(
            P(("groups", "pool"), None),
            P(),
            P(None, "pool"),
            P(None, ("groups", "pool")),
            P("groups", "pool"),
            P(("groups", "pool")),
            P(("groups", "pool")),
        ),
        out_specs=P("groups", "pool"),
        check_vma=False,
    )
```
